512 devices in a mesh: seq: 64 (over z_hi, y, core), head: 8 (over x, z_lo).
Axes of the slice: x: 4, y: 8, z: 8 (z_hi: 4, z_lo: 2; z = z_hi * 2 + z_lo), core: 2. Of those that a mesh axis runs over, the one named last changes fastest.
Arguments:
- query_rows: bfloat16 [32768, 8192], P('seq', 'head'), may hold values from -12 to 12
- key_rows: bfloat16 [32768, 1024], P(('seq', 'head')), may hold values from -6 to 6
- value_rows: bfloat16 [32768, 1024], P(('seq', 'head')), may hold values from -6 to 6
- tree_mask: int32 [64, 5], P('seq'), may hold values from 0 to 1, as said below
- token_depth: int32 [32768], P('seq'), may hold values from 0 to 7
Outputs:
- attended: bfloat16 [32768, 8192], P('seq', 'head')
- log_sums: float32 [64, 32768], P('head', 'seq')
The draws below stay inside these ranges and needn't reach their ends.
Inputs may be any that keep to these rules, and one draw needn't show every extreme that they name: `tree_mask`: column 0 of every row is 1; entry (i, s) is 0 where i < s.
All inputs are finite; a program needn't handle non-finite values.
Results may differ from the reference program's by a relative error of at most 0.0031.
Values may be sent and summed in bfloat16 or wider, within the bound.
A program may use at most 64 MiB of HBM per device.

```python
import jax
import jax.numpy as jnp
from jax import lax

HQ = 64
KVH = 8
HD = 128
BLOCK = 512
REACH = 4
DEPTHS = 8
NB = 64
TOKENS = 32768


def drawn_rows(key, strength):
    base_rows = jnp.clip(jax.random.normal(key, (TOKENS, KVH * HD), jnp.float32), -6.0, 6.0)
    token_index = jnp.arange(TOKENS)
    last_row = (token_index % BLOCK == BLOCK - 1).astype(jnp.float32) * strength
    key_out = base_rows * (1.0 - last_row)[:, None]
    return (key_out, last_row)


def draw_key_rows(key, part):
    strength = 0.0
    key_out, last_row = drawn_rows(key, strength)
    return key_out.astype(jnp.bfloat16)


def draw_query_rows(key, part):
    strength = 0.0
    key_out, last_row = drawn_rows(key, strength)
    key = jax.random.fold_in(key, 3)
    base_rows = jnp.clip(2.5 * jax.random.normal(key, (TOKENS, HQ * HD), jnp.float32), -12.0, 12.0)
    query_out = base_rows * (1.0 - last_row)[:, None]
    return query_out.astype(jnp.bfloat16)


def draw_tree_mask(key, part):
    key = jax.random.fold_in(key, 5)
    random_bits = jax.random.randint(key, (NB, REACH + 1), 0, 2)
    block_index = jnp.arange(NB)[:, None]
    offset = jnp.arange(REACH + 1)[None, :]
    random_bits = jnp.where(offset == 0, 1, random_bits)
    return jnp.where(block_index < offset, 0, random_bits).astype(jnp.int32)


def set_ends(drawn, own_key, low, largest):
    shape = drawn.shape
    spot = [jax.random.randint(jax.random.fold_in(own_key, axis), (), 0, shape[axis]) for axis in range(len(shape))]
    drawn = drawn.at[tuple(spot)].set(low)
    longest = shape.index(max(shape))
    spot[longest] = (spot[longest] + 1) % shape[longest]
    return drawn.at[tuple(spot)].set(largest)


def block_scale(own_key, shape, pieces, low, high):
    def one(dim, shards_of):
        heights = jax.random.uniform(jax.random.fold_in(jax.random.fold_in(own_key, 6), dim), (shards_of,), jnp.float32, low / len(pieces), high / len(pieces))
        return jnp.repeat(jnp.exp(heights), shape[dim] // shards_of).reshape((-1,) + (1,) * (len(shape) - dim - 1))

    level = one(*pieces[0])
    for cut in pieces[1:]:
        level = level * one(*cut)
    return level


def centred(rng, shape, spread, most, split=(), kind=jnp.bfloat16):
    loudness = block_scale(rng, shape, split, -0.22, 0.18) if split else 1.0
    result = jax.random.normal(rng, shape, jnp.float32) * spread * loudness
    return jnp.minimum(jnp.maximum(result, -most), most).astype(kind)


def setup_inputs(seed: int = 0) -> dict:
    seeds = jax.random.split(jax.random.key(seed), 6)
    return {
        "query_rows": draw_query_rows(jax.random.fold_in(seeds[5], 71), 0),
        "key_rows": draw_key_rows(jax.random.fold_in(seeds[5], 71), 0),
        "value_rows": centred(seeds[2], (TOKENS, KVH * HD), 1.0, 6.0, ((0, 512),)),
        "tree_mask": draw_tree_mask(jax.random.fold_in(seeds[5], 71), 0),
        "token_depth": set_ends(jax.random.randint(seeds[4], (TOKENS,), 0, DEPTHS), jax.random.fold_in(seeds[4], 1), 0, DEPTHS - 1).astype(jnp.int32),
    }


def reference(query_rows, key_rows, value_rows, tree_mask, token_depth):
    group_size = HQ // KVH
    score_scale = HD ** -0.5
    query_all = query_rows.reshape(NB, BLOCK, KVH, group_size, HD)
    key_all = jnp.concatenate([jnp.zeros((REACH * BLOCK, KVH * HD), key_rows.dtype), key_rows], 0).reshape(NB + REACH, BLOCK, KVH, HD)
    value_all = jnp.concatenate([jnp.zeros((REACH * BLOCK, KVH * HD), value_rows.dtype), value_rows], 0).reshape(NB + REACH, BLOCK, KVH, HD)
    depth_all = jnp.concatenate([jnp.zeros((REACH * BLOCK,), jnp.int32), token_depth.astype(jnp.int32)], 0).reshape(NB + REACH, BLOCK)
    position = jnp.arange(BLOCK)

    def one_block(block_index):
        block_start = block_index.astype(jnp.int32)
        key_window = lax.dynamic_slice_in_dim(key_all, block_start, REACH + 1, 0)
        value_window = lax.dynamic_slice_in_dim(value_all, block_start, REACH + 1, 0)
        depth_window = lax.dynamic_slice_in_dim(depth_all, block_start, REACH + 1, 0)
        depth_query = lax.dynamic_slice_in_dim(depth_all, block_start + REACH, 1, 0)[0]
        query_block = lax.dynamic_slice_in_dim(query_all, block_start, 1, 0)[0]
        mask_line = lax.dynamic_slice_in_dim(tree_mask, block_start, 1, 0)[0]
        allowed = mask_line[::-1] > 0
        causal = position[None, :] <= position[:, None]
        deeper = depth_window[None, :, :] <= depth_query[:, None, None]
        own_block = (jnp.arange(REACH + 1) == REACH)[None, :, None]
        visible = allowed[None, :, None] & jnp.where(own_block, causal[:, None, :], deeper)
        scores = jnp.einsum('qgch,jkgh->gcqjk', query_block.astype(jnp.float32), key_window.astype(jnp.float32)) * score_scale
        masked = jnp.where(visible[None, None], scores, -jnp.inf)
        row_top = jnp.max(masked, axis=(3, 4))
        exp_terms = jnp.exp(masked - row_top[..., None, None])
        row_total = jnp.sum(exp_terms, axis=(3, 4))
        weights = exp_terms.astype(jnp.bfloat16)
        mixed_rows = jnp.einsum('gcqjk,jkgh->qgch', weights.astype(jnp.float32), value_window.astype(jnp.float32))
        mixed_rows = mixed_rows / jnp.transpose(row_total, (2, 0, 1))[..., None]
        out_rows = mixed_rows.astype(jnp.bfloat16).reshape(BLOCK, HQ * HD)
        lse_rows = (row_top + jnp.log(row_total)).reshape(HQ, BLOCK)
        return out_rows, lse_rows

    attended, log_parts = lax.map(one_block, jnp.arange(NB, dtype=jnp.int32))
    log_sums = jnp.transpose(log_parts, (1, 0, 2)).reshape(HQ, TOKENS)
    return attended.reshape(TOKENS, HQ * HD), log_sums
```

```python
import functools

import jax
import jax.numpy as jnp
from jax import lax
from jax.experimental import pallas as pl
from jax.experimental.pallas import tpu as pltpu
from jax.sharding import PartitionSpec as P

HD = 128
BLOCK = 512
SLOTS = 5
GROUP = 8
HEADS = 8
ROWS = BLOCK // GROUP
DROWS = 16
KROWS = BLOCK + DROWS
CHIP = 2
YSIZE = 8
PLANE = CHIP * YSIZE
SCALE = float(HD**-0.5)
SCALE_LOG2 = float(HD**-0.5 * 1.4426950408889634)
HIDE = -(2.0**100)
MESH = pl.DeviceIdType.MESH
F32 = jnp.float32
BF16 = jnp.bfloat16
CONTRACT_LAST = (((1,), (1,)), ((), ()))


def lane_max(scores):
    best = scores[:, :HD]
    for j in range(1, scores.shape[1] // HD):
        best = jnp.maximum(best, scores[:, j * HD : (j + 1) * HD])
    return best


def kernel(
    blocks, q_hbm, k_hbm, v_hbm, mask_ref, depth_ref, o_ref, l_ref,
    qb, kb, vb, stage_k, stage_v, kx, qx, sc, mx, acc,
    k_send, k_recv, v_send, v_recv, local_sem,
):
    s = lax.axis_index("seq")
    g = lax.axis_index("head")
    core = s % CHIP
    other = s + 1 - 2 * core
    y = (s // CHIP) % YSIZE
    last_y = y == YSIZE - 1
    has_next = s < blocks - CHIP
    has_prev = s >= CHIP
    to_plane = last_y & has_next
    from_plane = last_y & (s >= PLANE)
    cross_in = (y == 0) & (s >= PLANE)

    def at_seq(t):
        return {"seq": t, "head": g}

    barrier = pltpu.get_barrier_semaphore()
    for j in range(1, GROUP):
        pl.semaphore_signal(
            barrier, inc=1, device_id={"seq": s, "head": (g + j) % GROUP}, device_id_type=MESH
        )
    pl.semaphore_signal(barrier, inc=1, device_id=at_seq(other), device_id_type=MESH)
    partners = (
        (has_next, s + CHIP),
        (has_prev, s - CHIP),
        (to_plane, s + PLANE),
        (from_plane, s - PLANE),
        (from_plane, s - PLANE + CHIP),
        (cross_in, s + PLANE - CHIP),
    )
    expected = jnp.int32(GROUP)
    for cond, target in partners:
        expected = expected + jnp.where(cond, 1, 0)

        @pl.when(cond)
        def _(target=target):
            pl.semaphore_signal(barrier, inc=1, device_id=at_seq(target), device_id_type=MESH)

    q_copy = pltpu.make_async_copy(q_hbm, qb, local_sem.at[2])
    q_copy.start()
    depth = depth_ref[...]
    depth_rows = jnp.concatenate(
        [depth[:, i * HD : (i + 1) * HD] for i in range(BLOCK // HD)]
        + [jnp.zeros((DROWS - BLOCK // HD, HD), jnp.int32)],
        0,
    )
    kb[0, BLOCK:] = depth_rows.astype(F32).astype(BF16)
    pl.semaphore_wait(barrier, expected)

    mine = pl.ds(pl.multiple_of(g * ROWS, ROWS), ROWS)

    def spread(src, dst, send, recv, lsem):
        copies = []
        for j in range(1, GROUP):
            t = (g + j) % GROUP
            copy = pltpu.make_async_remote_copy(
                src_ref=src.at[:, pl.ds(pl.multiple_of(t * HD, HD), HD)],
                dst_ref=dst.at[0, mine],
                send_sem=send.at[j - 1],
                recv_sem=recv.at[j - 1],
                device_id={"seq": s, "head": t},
                device_id_type=MESH,
            )
            copy.start()
            copies.append(copy)
        own = pltpu.make_async_copy(
            src.at[:, pl.ds(pl.multiple_of(g * HD, HD), HD)], dst.at[0, mine], lsem
        )
        own.start()
        return copies, own

    k_spread, k_own = spread(k_hbm, kb, k_send, k_recv, local_sem.at[0])
    v_spread, v_own = spread(v_hbm, vb, v_send, v_recv, local_sem.at[1])

    def moves(buf, stage, send, recv):
        def move(src, dst, i, target):
            return pltpu.make_async_remote_copy(
                src_ref=src,
                dst_ref=dst,
                send_sem=send.at[i],
                recv_sem=recv.at[i],
                device_id=at_seq(target),
                device_id_type=MESH,
            )

        return dict(
            hop1=move(buf.at[0], buf.at[2], 7, s + CHIP),
            hop2=move(buf.at[2], buf.at[4], 9, s + CHIP),
            plane=move(buf.at[2], stage, 11, s + PLANE),
            cross=move(stage, buf.at[4], 9, s - PLANE + CHIP),
            one_a=move(buf.at[0], buf.at[1], 8, other),
            one_b=move(buf.at[2], buf.at[1], 8, other),
            three_a=move(buf.at[2], buf.at[3], 10, other),
            three_b=move(buf.at[4], buf.at[3], 10, other),
        )

    km = moves(kb, stage_k, k_send, k_recv)
    vm = moves(vb, stage_v, v_send, v_recv)

    def when(cond, act):
        @pl.when(cond)
        def _():
            act()

    core0, core1 = core == 0, core == 1
    fwd = has_prev & has_next & jnp.logical_not(last_y)
    fwd_plane = to_plane

    def send_first(m):
        when(has_next, m["hop1"].start)
        when(core0, m["one_a"].start)

    def pass_second(m):
        when(has_prev, m["hop1"].wait_recv)
        when(fwd, m["hop2"].start)
        when(fwd_plane, m["plane"].start)
        when(core0 & has_prev, m["three_a"].start)
        when(core1 & has_prev, m["one_b"].start)

    def pass_fourth(m):
        when(s >= 4, m["hop2"].wait_recv)
        when(core1 & (s >= 4), m["three_b"].start)

    def pass_plane(m):
        def act():
            m["plane"].wait_recv()
            m["cross"].start()

        when(from_plane, act)

    q_copy.wait()
    sub = lax.broadcasted_iota(jnp.int32, (HD, BLOCK), 0)
    q_side = jnp.where(
        sub < 8, jnp.where(sub > depth, HIDE, 0.0), jnp.where(sub == 8, 1.0, 0.0)
    ).astype(F32)
    qx[...] = q_side.T.astype(BF16)

    def key_side(slot):
        rows = kb[slot, BLOCK:, :].astype(F32)
        line = jnp.concatenate([rows[i : i + 1] for i in range(BLOCK // HD)], 1)
        off = jnp.where(mask_ref[0, slot] > 0, 0.0, HIDE).astype(F32)
        side = jnp.where(
            sub < 8, jnp.where(sub.astype(F32) == line, 1.0, 0.0), jnp.where(sub == 8, off, 0.0)
        ).astype(F32)
        kx[...] = side.T.astype(BF16)

    half = BLOCK // 2

    def own_scores():
        row = lax.broadcasted_iota(jnp.int32, (half, half), 0)
        col = lax.broadcasted_iota(jnp.int32, (half, half), 1)

        def heads(i, carry):
            for k in range(4):
                h = i * 4 + k
                cols = pl.ds(pl.multiple_of(h * HD, HD), HD)
                for t in range(2):
                    rs = slice(t * half, (t + 1) * half)
                    n = (t + 1) * half
                    scores = lax.dot_general(
                        qb[rs, cols], kb[0, :n], CONTRACT_LAST, preferred_element_type=F32
                    )
                    diag = jnp.where(col <= row, scores[:, n - half :], HIDE)
                    sc[h, 0, rs, n - half : n] = diag
                    best = lane_max(diag)
                    if t:
                        sc[h, 0, rs, : n - half] = scores[:, : n - half]
                        best = jnp.maximum(best, lane_max(scores[:, : n - half]))
                    mx[h, rs] = best
            return carry

        lax.fori_loop(0, HEADS // 4, heads, 0)

    def slot_scores(slot):
        key_side(slot)

        def heads(i, carry):
            keys = jnp.concatenate([kb[slot, :BLOCK], kx[...]], 1)
            for k in range(4):
                h = i * 4 + k
                cols = pl.ds(pl.multiple_of(h * HD, HD), HD)
                query = jnp.concatenate([qb[:, cols], qx[...]], 1)
                scores = lax.dot_general(query, keys, CONTRACT_LAST, preferred_element_type=F32)
                sc[h, slot] = scores
                mx[h] = jnp.maximum(mx[h], lane_max(scores))
            return carry

        lax.fori_loop(0, HEADS // 4, heads, 0)

    def wait_spread(copies, own):
        own.wait()
        for copy in copies:
            copy.wait_recv()

    wait_spread(k_spread, k_own)
    send_first(km)
    own_scores()
    pass_second(km)
    wait_spread(v_spread, v_own)
    send_first(vm)

    for slot in range(1, SLOTS):

        @pl.when(s < slot)
        def _(slot=slot):
            vb[slot] = jnp.zeros((BLOCK, HD), BF16)

            def fill(h, carry):
                sc[h, slot] = jnp.full((BLOCK, BLOCK), HIDE, F32)
                return carry

            lax.fori_loop(0, HEADS, fill, 0)

    when(core1, km["one_a"].wait_recv)
    second, third, fourth, fifth = 2 - core, 1 + core, 4 - core, 3 + core
    when(s >= second, lambda: slot_scores(second))
    when(core0 & (s >= 1), km["one_a"].wait_recv)
    when(s >= third, lambda: slot_scores(third))
    pass_fourth(km)
    when(core1 & (s >= 3), km["three_a"].wait_recv)
    when(s >= fourth, lambda: slot_scores(fourth))
    pass_plane(km)
    pass_second(vm)
    when(core0 & (s >= 3), km["three_a"].wait_recv)
    when(s >= fifth, lambda: slot_scores(fifth))
    when(s >= 1, vm["one_a"].wait_recv)

    def attend(slots, first, last):
        def heads(i, carry):
            for k in range(2):
                h = i * 2 + k
                cols = pl.ds(pl.multiple_of(h * HD, HD), HD)
                for t in range(2):
                    rs = slice(t * half, (t + 1) * half)
                    if first:
                        top = jnp.max(mx[h, rs], axis=1, keepdims=True)
                        mx[h, rs] = jnp.broadcast_to(top, (half, HD))
                        total = jnp.zeros((half, 2 * HD), F32)
                    else:
                        top = mx[h, rs][:, :1]
                        total = acc[h, rs]
                    for slot in slots:
                        n = BLOCK if slot else (t + 1) * half
                        terms = jnp.exp2((sc[h, slot, rs, :n] - top) * SCALE_LOG2)
                        values = jnp.concatenate([vb[slot, :n], jnp.ones((n, HD), BF16)], 1)
                        total = total + jnp.dot(
                            terms.astype(BF16), values, preferred_element_type=F32
                        )
                    if last:
                        sums = total[:, HD:]
                        o_ref[rs, cols] = (total[:, :HD] / sums).astype(BF16)
                        logs = top * SCALE + jnp.log(sums[:, :1])
                        l_ref[pl.ds(h, 1), rs] = logs.reshape(1, half)
                    else:
                        acc[h, rs] = total
            return carry

        lax.fori_loop(0, HEADS // 2, heads, 0)

    attend((0, 1, 2), True, False)
    pass_fourth(vm)
    pass_plane(vm)
    when(s >= 3, vm["three_a"].wait_recv)
    attend((3, 4), False, True)

    for copy in k_spread + v_spread:
        copy.wait_send()
    for m in (km, vm):
        when(has_next, m["hop1"].wait_send)
        when(fwd, m["hop2"].wait_send)
        when(fwd_plane, m["plane"].wait_send)
        when(from_plane, m["cross"].wait_send)
        when(core0 | has_prev, m["one_a"].wait_send)
        when((core0 & has_prev) | (core1 & (s >= 4)), m["three_a"].wait_send)


def solution(mesh):
    blocks = mesh.shape["seq"]

    def body(query_rows, key_rows, value_rows, tree_mask, token_depth):
        vmem = pl.BlockSpec(memory_space=pltpu.VMEM)
        anywhere = pl.BlockSpec(memory_space=pl.ANY)
        sems = pltpu.SemaphoreType.DMA
        return pl.pallas_call(
            functools.partial(kernel, blocks),
            out_shape=(
                jax.ShapeDtypeStruct((BLOCK, HEADS * HD), BF16),
                jax.ShapeDtypeStruct((HEADS, BLOCK), F32),
            ),
            in_specs=[anywhere] * 3 + [pl.BlockSpec(memory_space=pltpu.SMEM), vmem],
            out_specs=(vmem, vmem),
            scratch_shapes=[
                pltpu.VMEM((BLOCK, HEADS * HD), BF16),
                pltpu.VMEM((SLOTS, KROWS, HD), BF16),
                pltpu.VMEM((SLOTS, BLOCK, HD), BF16),
                pltpu.VMEM((KROWS, HD), BF16),
                pltpu.VMEM((BLOCK, HD), BF16),
                pltpu.VMEM((BLOCK, HD), BF16),
                pltpu.VMEM((BLOCK, HD), BF16),
                pltpu.VMEM((HEADS, SLOTS, BLOCK, BLOCK), F32),
                pltpu.VMEM((HEADS, BLOCK, HD), F32),
                pltpu.VMEM((HEADS, BLOCK, 2 * HD), F32),
                sems((12,)), sems((12,)), sems((12,)), sems((12,)), sems((3,)),
            ],
            compiler_params=pltpu.CompilerParams(
                collective_id=0, has_side_effects=True, vmem_limit_bytes=60 * 2**20
            ),
        )(query_rows, key_rows, value_rows, tree_mask, token_depth.reshape(1, BLOCK))

    return jax.shard_map(
        body,
        mesh=mesh,
        in_specs=(
            P("seq", "head"),
            P(("seq", "head"), None),
            P(("seq", "head"), None),
            P("seq", None),
            P("seq"),
        ),
        out_specs=(P("seq", "head"), P("head", "seq")),
        check_vma=False,
    )
```

```python
import functools

import jax
import jax.numpy as jnp
from jax import lax
from jax.experimental import pallas as pl
from jax.experimental.pallas import tpu as pltpu
from jax.sharding import PartitionSpec as P

HD = 128
BLOCK = 512
SLOTS = 5
GROUP = 8
HEADS = 8
PER_BODY = 8
PIECES = 4
ROWS = BLOCK // GROUP
HALF = BLOCK // 2
DROWS = 16
KROWS = BLOCK + DROWS
CHIP = 2
YSIZE = 8
PLANE = CHIP * YSIZE
SCALE = float(HD**-0.5)
SCALE_LOG2 = float(HD**-0.5 * 1.4426950408889634)
HIDE = -(2.0**100)
MESH = pl.DeviceIdType.MESH
F32 = jnp.float32
BF16 = jnp.bfloat16
CONTRACT_LAST = (((1,), (1,)), ((), ()))


def lane_max(scores):
    best = scores[:, :HD]
    for j in range(1, scores.shape[1] // HD):
        best = jnp.maximum(best, scores[:, j * HD : (j + 1) * HD])
    return best


def kernel(
    blocks, q_hbm, k_hbm, v_hbm, mask_hbm, depth_hbm, o_hbm, l_ref,
    mask_ref, depth_ref, k_in, v_in, ob, qb, kb, vb, kx, qx, sc, mx, tops, acc,
    k_send, k_recv, v_send, v_recv, local_sem,
):
    s = lax.axis_index("seq")
    g = lax.axis_index("head")
    core = s % CHIP
    other = s + 1 - 2 * core
    y = (s // CHIP) % YSIZE
    last_y = y == YSIZE - 1
    has_next = s < blocks - CHIP
    has_prev = s >= CHIP
    core0, core1 = core == 0, core == 1
    skips = last_y & core0 & has_next
    hands_back = (y == 1) & core0 & (s >= PLANE)
    relayed = (y == 0) & core0 & has_prev
    passes = has_prev & has_next & jnp.logical_not(relayed)

    def at_seq(t):
        return {"seq": t, "head": g}

    barrier = pltpu.get_barrier_semaphore()
    for j in range(1, GROUP):
        pl.semaphore_signal(
            barrier, inc=1, device_id={"seq": s, "head": (g + j) % GROUP}, device_id_type=MESH
        )
    pl.semaphore_signal(barrier, inc=1, device_id=at_seq(other), device_id_type=MESH)
    partners = (
        (has_next, s + CHIP),
        (has_prev, s - CHIP),
        (skips, s + 2 * CHIP),
        (hands_back, s - 2 * CHIP),
        (core1 & has_next, s + CHIP - 1),
        (core0 & has_prev, s - CHIP + 1),
    )
    expected = jnp.int32(GROUP)
    for cond, target in partners:
        expected = expected + jnp.where(cond, 1, 0)

        @pl.when(cond)
        def _(target=target):
            pl.semaphore_signal(barrier, inc=1, device_id=at_seq(target), device_id_type=MESH)

    q_copy = pltpu.make_async_copy(q_hbm, qb, local_sem.at[2])
    mask_copy = pltpu.make_async_copy(mask_hbm, mask_ref, local_sem.at[3])
    depth_copy = pltpu.make_async_copy(depth_hbm, depth_ref, local_sem.at[4])
    k_in_copy = pltpu.make_async_copy(k_hbm, k_in, local_sem.at[7])
    v_in_copy = pltpu.make_async_copy(v_hbm, v_in, local_sem.at[8])
    depth_copy.start()
    mask_copy.start()
    k_in_copy.start()
    v_in_copy.start()
    q_copy.start()
    depth_copy.wait()
    mask_copy.wait()
    depth = depth_ref[...]
    depth_rows = jnp.concatenate(
        [depth[:, i * HD : (i + 1) * HD] for i in range(BLOCK // HD)]
        + [jnp.zeros((DROWS - BLOCK // HD, HD), jnp.int32)],
        0,
    )
    kb[0, BLOCK:] = depth_rows.astype(F32).astype(BF16)
    k_in_copy.wait()
    v_in_copy.wait()
    pl.semaphore_wait(barrier, expected)

    mine = pl.ds(pl.multiple_of(g * ROWS, ROWS), ROWS)

    def spread(src, dst, send, recv, lsem):
        copies = []
        for j in range(1, GROUP):
            t = (g + j) % GROUP
            copy = pltpu.make_async_remote_copy(
                src_ref=src.at[:, pl.ds(pl.multiple_of(t * HD, HD), HD)],
                dst_ref=dst.at[0, mine],
                send_sem=send.at[j - 1],
                recv_sem=recv.at[j - 1],
                device_id={"seq": s, "head": t},
                device_id_type=MESH,
            )
            copy.start()
            copies.append(copy)
        own = pltpu.make_async_copy(
            src.at[:, pl.ds(pl.multiple_of(g * HD, HD), HD)], dst.at[0, mine], lsem
        )
        own.start()
        return copies, own

    k_spread, k_own = spread(k_in, kb, k_send, k_recv, local_sem.at[0])
    v_spread, v_own = spread(v_in, vb, v_send, v_recv, local_sem.at[1])

    far = jnp.where(skips, 1, 0)
    ahead = s + CHIP + CHIP * far

    def moves(buf, send, recv, parts):
        def move(src, rows, dst, i, at, target):
            return pltpu.make_async_remote_copy(
                src_ref=buf.at[src, rows],
                dst_ref=buf.at[dst, rows],
                send_sem=send.at[i],
                recv_sem=recv.at[at],
                device_id=at_seq(target),
                device_id_type=MESH,
            )

        whole = pl.ds(0, buf.shape[1])
        each = list(enumerate(parts))
        return dict(
            one_a=move(0, whole, 1, 13, 13, other),
            one_b=move(2, whole, 1, 13, 13, other),
            three_a=move(2, whole, 3, 14, 14, other),
            four=move(3, whole, 4, 15, 15, other),
            hop1=[move(0, p, 2 + 2 * far, 7 + i, 7 + i + 2 * far, ahead) for i, p in each],
            hop2=[move(2, p, 4 - core, 9 + i, 9 + i + 2 * core, s + CHIP - core) for i, p in each],
            in3=[move(2, p, 3, 9 + i, 11 + i, s + CHIP) for i, p in each],
            in2=[move(0, p, 2, 7 + i, 7 + i, s + CHIP) for i, p in each],
            in4=[move(2, p, 4, 9 + i, 9 + i, s + CHIP) for i, p in each],
            back2=[move(4, p, 2, 11 + i, 7 + i, s - CHIP) for i, p in each],
        )

    km = moves(kb, k_send, k_recv, (pl.ds(0, HALF), pl.ds(HALF, KROWS - HALF)))
    vm = moves(vb, v_send, v_recv, (pl.ds(0, BLOCK),))

    def when(cond, act):
        @pl.when(cond)
        def _():
            act()

    def send_first(m):
        when(core0, m["one_a"].start)
        for copy in m["hop1"]:
            when(has_next, copy.start)

    def pass_second(m, later):
        for copy in m["in2"]:
            when(has_prev, copy.wait_recv)
        when(core0 & has_prev, m["three_a"].start)
        when(core1 & has_prev, m["one_b"].start)
        for copy in m["hop2"]:
            when(passes & jnp.logical_not(later), copy.start)

    def hand_back(m):
        for arrived, back in zip(m["in4"], m["back2"]):
            arrived.wait_recv()
            back.start()
        for copy in m["hop2"]:
            copy.start()

    def take_third(m):
        for copy in m["in3"]:
            copy.wait_recv()
        m["four"].start()

    def take_fourth(m):
        for copy in m["in4"]:
            when(core0 & (s >= 4) & jnp.logical_not(hands_back), copy.wait_recv)
        when(core1 & (s >= 4), m["four"].wait_recv)

    q_copy.wait()
    sub = lax.broadcasted_iota(jnp.int32, (HD, BLOCK), 0)
    q_side = jnp.where(
        sub < 8, jnp.where(sub > depth, HIDE, 0.0), jnp.where(sub == 8, 1.0, 0.0)
    ).astype(F32)
    qx[...] = q_side.T.astype(BF16)

    def key_side(slot):
        rows = kb[slot, BLOCK:, :].astype(F32)
        line = jnp.concatenate([rows[i : i + 1] for i in range(BLOCK // HD)], 1)
        off = jnp.where(mask_ref[0, slot] > 0, 0.0, HIDE).astype(F32)
        side = jnp.where(
            sub < 8, jnp.where(sub.astype(F32) == line, 1.0, 0.0), jnp.where(sub == 8, off, 0.0)
        ).astype(F32)
        kx[...] = side.T.astype(BF16)

    half = HALF

    def spread_max(scores):
        return jnp.broadcast_to(
            jnp.max(lane_max(scores), axis=1, keepdims=True), (scores.shape[0], HD)
        )

    def own_scores():
        row = lax.broadcasted_iota(jnp.int32, (half, half), 0)
        col = lax.broadcasted_iota(jnp.int32, (half, half), 1)

        def heads(i, carry):
            for k in range(PER_BODY):
                h = i * PER_BODY + k
                cols = pl.ds(pl.multiple_of(h * HD, HD), HD)
                for t in range(2):
                    rs = slice(t * half, (t + 1) * half)
                    n = (t + 1) * half
                    scores = lax.dot_general(
                        qb[rs, cols], kb[0, :n], CONTRACT_LAST, preferred_element_type=F32
                    )
                    diag = jnp.where(col <= row, scores[:, n - half :], HIDE)
                    sc[h, 0, rs, n - half : n] = diag
                    best = lane_max(diag)
                    if t:
                        sc[h, 0, rs, : n - half] = scores[:, : n - half]
                        best = jnp.maximum(best, lane_max(scores[:, : n - half]))
                    mx[h, rs] = spread_max(best)
            return carry

        lax.fori_loop(0, HEADS // PER_BODY, heads, 0)

    def slot_scores(slot):
        key_side(slot)

        def heads(i, carry):
            keys = jnp.concatenate([kb[slot, :BLOCK], kx[...]], 1)
            for k in range(PER_BODY):
                h = i * PER_BODY + k
                cols = pl.ds(pl.multiple_of(h * HD, HD), HD)
                query = jnp.concatenate([qb[:, cols], qx[...]], 1)
                scores = lax.dot_general(query, keys, CONTRACT_LAST, preferred_element_type=F32)
                sc[h, slot] = scores
                mx[h] = jnp.maximum(mx[h], spread_max(scores))
            return carry

        lax.fori_loop(0, HEADS // PER_BODY, heads, 0)

    def store_result(h, rs, sums, top):
        cols = pl.ds(pl.multiple_of(h * HD, HD), HD)
        ob[rs, cols] = (sums[:, :HD] / sums[:, HD:]).astype(BF16)
        logs = top * SCALE + jnp.log(sums[:, HD:])
        l_ref[pl.ds(h, 1), rs] = logs[:, :1].reshape(1, half)

    def out_copy(i):
        cols = pl.ds(pl.multiple_of(i * (HEADS * HD // 2), HEADS * HD // 2), HEADS * HD // 2)
        return pltpu.make_async_copy(ob.at[:, cols], o_hbm.at[:, cols], local_sem.at[5 + i])

    def absorb(slots, first=False, last=False):
        def heads(i, carry):
            for k in range(HEADS // 2):
                h = i * (HEADS // 2) + k
                for t in range(2):
                    rs = slice(t * half, (t + 1) * half)
                    top = mx[h, rs]
                    sums = None
                    for slot in slots:
                        n = (t + 1) * half if first else BLOCK
                        terms = jnp.concatenate(
                            [
                                jnp.exp2(
                                    (sc[h, slot, rs, j * HD : (j + 1) * HD] - top) * SCALE_LOG2
                                ).astype(BF16)
                                for j in range(n // HD)
                            ],
                            1,
                        )
                        values = jnp.concatenate([vb[slot, :n], jnp.ones((n, HD), BF16)], 1)
                        part = jnp.dot(terms, values, preferred_element_type=F32)
                        sums = part if sums is None else sums + part
                    if not first:
                        fade = jnp.exp2((tops[h, rs] - top) * SCALE_LOG2)
                        sums = acc[h, rs] * jnp.concatenate([fade, fade], 1) + sums
                    if last:
                        store_result(h, rs, sums, top)
                    else:
                        acc[h, rs] = sums
                        tops[h, rs] = top
            if last:
                out_copy(i).start()
            return carry

        lax.fori_loop(0, 2, heads, 0)

    def finish():
        def heads(i, carry):
            for k in range(HEADS // 2):
                h = i * (HEADS // 2) + k
                for t in range(2):
                    rs = slice(t * half, (t + 1) * half)
                    store_result(h, rs, acc[h, rs], tops[h, rs])
            out_copy(i).start()
            return carry

        lax.fori_loop(0, 2, heads, 0)

    def wait_spread(copies, own):
        own.wait()
        for copy in copies:
            copy.wait_recv()

    wait_spread(k_spread, k_own)
    send_first(km)
    own_scores()
    wait_spread(v_spread, v_own)
    send_first(vm)
    absorb((0,), first=True)

    @pl.when(s == 1)
    def _():
        vb[2] = jnp.zeros((BLOCK, HD), BF16)

        def fill(h, carry):
            sc[h, 2] = jnp.full((BLOCK, BLOCK), HIDE, F32)
            return carry

        lax.fori_loop(0, HEADS, fill, 0)

    def by_round(r, first_core, second_core):
        pick = jnp.int32(0)
        for i in range(len(first_core)):
            pick = jnp.where(r == i, jnp.where(core0, first_core[i], second_core[i]), pick)
        return pick

    def round_of(r, carry):
        def at(i, cond, act):
            when((r == i) & cond, act)

        plain0 = core0 & jnp.logical_not(relayed)
        at(0, core1, km["one_a"].wait_recv)
        at(1, jnp.logical_not(relayed), lambda: pass_second(km, hands_back))
        at(1, relayed, km["one_a"].wait_recv)
        at(2, hands_back, lambda: hand_back(km))
        at(2, relayed, lambda: pass_second(km, hands_back))
        at(2, jnp.logical_not(relayed), lambda: pass_second(vm, hands_back | skips))
        at(2, plain0 & (s >= 1), km["one_a"].wait_recv)
        at(3, hands_back, lambda: hand_back(vm))
        at(3, core0 & (s >= 4), lambda: take_third(km))
        at(3, core1 & (s >= 3), vm["three_a"].wait_recv)
        at(4, skips & passes, vm["hop2"][0].start)
        at(4, relayed, lambda: pass_second(vm, hands_back))
        at(5, core0 & (s >= 4), lambda: take_third(vm))
        pairs = (r == jnp.where(core1, 2, jnp.where(relayed, 4, 5))) & (s >= 1)
        when(pairs, vm["one_a"].wait_recv)
        when(pairs, lambda: absorb((1, 2)))
        thirds = ((r == 3) & core1 & (s >= 3)) | ((r == 5) & relayed)
        when(thirds, lambda: absorb((3,)))
        at(2, core1 & (s >= 3), km["three_a"].wait_recv)
        at(3, core1, lambda: take_fourth(km))
        at(4, core0, lambda: take_fourth(km))
        slot = by_round(
            r,
            tuple(jnp.where(relayed, i, j) for i, j in ((0, 0), (1, 2), (2, 1), (3, 3), (4, 4))),
            (1, 2, 3, 4, 0),
        )

        @pl.when((slot > 0) & (slot <= s))
        def _():
            slot_scores(slot)

        return carry

    lax.fori_loop(0, 6, round_of, 0)
    take_fourth(vm)
    both = core0 & jnp.logical_not(relayed)
    when((s >= 4) & both, lambda: absorb((3, 4), last=True))
    when((s >= 4) & jnp.logical_not(both), lambda: absorb((4,), last=True))
    when(s < 4, finish)
    for i in range(2):
        out_copy(i).wait()

    for copy in k_spread + v_spread:
        copy.wait_send()
    for m in (km, vm):
        for i in range(len(m["hop1"])):
            when(has_next, m["hop1"][i].wait_send)
            when(passes, m["hop2"][i].wait_send)
            when(hands_back, m["back2"][i].wait_send)
        when(core0 | has_prev, m["one_a"].wait_send)
        when(core0 & has_prev, m["three_a"].wait_send)
        when(core0 & (s >= 4), m["four"].wait_send)


def copy_out(a_in, l_in, a_out, l_out, a_buf, l_buf, sem_in, sem_out):
    rows = BLOCK // PIECES
    pieces = [pl.ds(i * rows, rows) for i in range(PIECES)]
    loads = [
        pltpu.make_async_copy(a_in.at[p], a_buf.at[p], sem_in.at[i]) for i, p in enumerate(pieces)
    ] + [pltpu.make_async_copy(l_in, l_buf, sem_in.at[PIECES])]
    stores = [
        pltpu.make_async_copy(a_buf.at[p], a_out.at[p], sem_out.at[i])
        for i, p in enumerate(pieces)
    ] + [pltpu.make_async_copy(l_buf, l_out, sem_out.at[PIECES])]
    for load in loads:
        load.start()
    for load, store in zip(loads, stores):
        load.wait()
        store.start()
    for store in stores:
        store.wait()


def solution(mesh):
    blocks = mesh.shape["seq"]

    def body(query_rows, key_rows, value_rows, tree_mask, token_depth):
        vmem = pl.BlockSpec(memory_space=pltpu.VMEM)
        anywhere = pl.BlockSpec(memory_space=pl.ANY)
        sems = pltpu.SemaphoreType.DMA
        results = pl.pallas_call(
            functools.partial(kernel, blocks),
            out_shape=(
                jax.ShapeDtypeStruct((BLOCK, HEADS * HD), BF16),
                jax.ShapeDtypeStruct((HEADS, BLOCK), F32),
            ),
            in_specs=[anywhere] * 5,
            out_specs=(anywhere, vmem),
            scratch_shapes=[
                pltpu.SMEM((1, SLOTS), jnp.int32),
                pltpu.VMEM((1, BLOCK), jnp.int32),
                pltpu.VMEM((ROWS, GROUP * HD), BF16),
                pltpu.VMEM((ROWS, GROUP * HD), BF16),
                pltpu.VMEM((BLOCK, HEADS * HD), BF16),
                pltpu.VMEM((BLOCK, HEADS * HD), BF16),
                pltpu.VMEM((SLOTS, KROWS, HD), BF16),
                pltpu.VMEM((SLOTS, BLOCK, HD), BF16),
                pltpu.VMEM((BLOCK, HD), BF16),
                pltpu.VMEM((BLOCK, HD), BF16),
                pltpu.VMEM((HEADS, SLOTS, BLOCK, BLOCK), F32),
                pltpu.VMEM((HEADS, BLOCK, HD), F32),
                pltpu.VMEM((HEADS, BLOCK, HD), F32),
                pltpu.VMEM((HEADS, BLOCK, 2 * HD), F32),
                sems((16,)), sems((16,)), sems((16,)), sems((16,)), sems((9,)),
            ],
            compiler_params=pltpu.CompilerParams(
                collective_id=0, has_side_effects=True, vmem_limit_bytes=60 * 2**20
            ),
        )(query_rows, key_rows, value_rows, tree_mask, token_depth.reshape(1, BLOCK))
        return pl.pallas_call(
            copy_out,
            out_shape=tuple(jax.ShapeDtypeStruct(r.shape, r.dtype) for r in results),
            in_specs=[anywhere] * 2,
            out_specs=(anywhere,) * 2,
            scratch_shapes=[
                pltpu.VMEM((BLOCK, HEADS * HD), BF16),
                pltpu.VMEM((HEADS, BLOCK), F32),
                sems((PIECES + 1,)),
                sems((PIECES + 1,)),
            ],
            compiler_params=pltpu.CompilerParams(vmem_limit_bytes=60 * 2**20),
        )(*results)

    return jax.shard_map(
        body,
        mesh=mesh,
        in_specs=(
            P("seq", "head"),
            P(("seq", "head"), None),
            P(("seq", "head"), None),
            P("seq", None),
            P("seq"),
        ),
        out_specs=(P("seq", "head"), P("head", "seq")),
        check_vma=False,
    )
```

```python
import functools

import jax
import jax.numpy as jnp
from jax import lax
from jax.experimental import pallas as pl
from jax.experimental.pallas import tpu as pltpu
from jax.sharding import PartitionSpec as P

HD = 128
BLOCK = 512
SLOTS = 5
GROUP = 8
HEADS = 8
PER_BODY = 8
PIECES = 4
ROWS = BLOCK // GROUP
HALF = BLOCK // 2
DROWS = 16
KROWS = BLOCK + DROWS
CHIP = 2
YSIZE = 8
PLANE = CHIP * YSIZE
SCALE = float(HD**-0.5)
SCALE_LOG2 = float(HD**-0.5 * 1.4426950408889634)
HIDE = -(2.0**100)
MESH = pl.DeviceIdType.MESH
F32 = jnp.float32
BF16 = jnp.bfloat16
CONTRACT_LAST = (((1,), (1,)), ((), ()))


def lane_max(scores):
    best = scores[:, :HD]
    for j in range(1, scores.shape[1] // HD):
        best = jnp.maximum(best, scores[:, j * HD : (j + 1) * HD])
    return best


def kernel(
    blocks, q_hbm, k_hbm, v_hbm, mask_hbm, depth_hbm, o_hbm, l_ref,
    mask_ref, depth_ref, k_in, v_in, ob, qb, kb, vb, kx, qx, sc, mx, tops, acc,
    k_send, k_recv, v_send, v_recv, local_sem,
):
    s = lax.axis_index("seq")
    g = lax.axis_index("head")
    core = s % CHIP
    other = s + 1 - 2 * core
    y = (s // CHIP) % YSIZE
    last_y = y == YSIZE - 1
    has_next = s < blocks - CHIP
    has_prev = s >= CHIP
    core0, core1 = core == 0, core == 1
    skips = last_y & core0 & has_next
    hands_back = (y == 1) & core0 & (s >= PLANE)
    relayed = (y == 0) & core0 & has_prev
    passes = has_prev & has_next & jnp.logical_not(relayed)

    def at_seq(t):
        return {"seq": t, "head": g}

    barrier = pltpu.get_barrier_semaphore()
    for j in range(1, GROUP):
        pl.semaphore_signal(
            barrier, inc=1, device_id={"seq": s, "head": (g + j) % GROUP}, device_id_type=MESH
        )
    pl.semaphore_signal(barrier, inc=1, device_id=at_seq(other), device_id_type=MESH)
    partners = (
        (has_next, s + CHIP),
        (has_prev, s - CHIP),
        (skips, s + 2 * CHIP),
        (hands_back, s - 2 * CHIP),
        (core1 & has_next, s + CHIP - 1),
        (core0 & has_prev, s - CHIP + 1),
    )
    expected = jnp.int32(GROUP)
    for cond, target in partners:
        expected = expected + jnp.where(cond, 1, 0)

        @pl.when(cond)
        def _(target=target):
            pl.semaphore_signal(barrier, inc=1, device_id=at_seq(target), device_id_type=MESH)

    q_copy = pltpu.make_async_copy(q_hbm, qb, local_sem.at[2])
    mask_copy = pltpu.make_async_copy(mask_hbm, mask_ref, local_sem.at[3])
    depth_copy = pltpu.make_async_copy(depth_hbm, depth_ref, local_sem.at[4])
    k_in_copy = pltpu.make_async_copy(k_hbm, k_in, local_sem.at[7])
    v_in_copy = pltpu.make_async_copy(v_hbm, v_in, local_sem.at[8])
    depth_copy.start()
    mask_copy.start()
    k_in_copy.start()
    v_in_copy.start()
    q_copy.start()
    depth_copy.wait()
    mask_copy.wait()
    depth = depth_ref[...]
    depth_rows = jnp.concatenate(
        [depth[:, i * HD : (i + 1) * HD] for i in range(BLOCK // HD)]
        + [jnp.zeros((DROWS - BLOCK // HD, HD), jnp.int32)],
        0,
    )
    kb[0, BLOCK:] = depth_rows.astype(F32).astype(BF16)
    k_in_copy.wait()
    v_in_copy.wait()
    pl.semaphore_wait(barrier, expected)

    mine = pl.ds(pl.multiple_of(g * ROWS, ROWS), ROWS)

    def spread(src, dst, send, recv, lsem):
        copies = []
        for j in range(1, GROUP):
            t = (g + j) % GROUP
            copy = pltpu.make_async_remote_copy(
                src_ref=src.at[:, pl.ds(pl.multiple_of(t * HD, HD), HD)],
                dst_ref=dst.at[0, mine],
                send_sem=send.at[j - 1],
                recv_sem=recv.at[j - 1],
                device_id={"seq": s, "head": t},
                device_id_type=MESH,
            )
            copy.start()
            copies.append(copy)
        own = pltpu.make_async_copy(
            src.at[:, pl.ds(pl.multiple_of(g * HD, HD), HD)], dst.at[0, mine], lsem
        )
        own.start()
        return copies, own

    k_spread, k_own = spread(k_in, kb, k_send, k_recv, local_sem.at[0])
    v_spread, v_own = spread(v_in, vb, v_send, v_recv, local_sem.at[1])

    far = jnp.where(skips, 1, 0)
    ahead = s + CHIP + CHIP * far

    def moves(buf, send, recv, parts):
        def move(src, rows, dst, i, at, target):
            return pltpu.make_async_remote_copy(
                src_ref=buf.at[src, rows],
                dst_ref=buf.at[dst, rows],
                send_sem=send.at[i],
                recv_sem=recv.at[at],
                device_id=at_seq(target),
                device_id_type=MESH,
            )

        whole = pl.ds(0, buf.shape[1])
        each = list(enumerate(parts))
        return dict(
            one_a=move(0, whole, 1, 13, 13, other),
            one_b=move(2, whole, 1, 13, 13, other),
            three_a=move(2, whole, 3, 14, 14, other),
            four=move(3, whole, 4, 15, 15, other),
            hop1=[move(0, p, 2 + 2 * far, 7 + i, 7 + i + 2 * far, ahead) for i, p in each],
            hop2=[move(2, p, 4 - core, 9 + i, 9 + i + 2 * core, s + CHIP - core) for i, p in each],
            in3=[move(2, p, 3, 9 + i, 11 + i, s + CHIP) for i, p in each],
            in2=[move(0, p, 2, 7 + i, 7 + i, s + CHIP) for i, p in each],
            in4=[move(2, p, 4, 9 + i, 9 + i, s + CHIP) for i, p in each],
            back2=[move(4, p, 2, 11 + i, 7 + i, s - CHIP) for i, p in each],
        )

    km = moves(kb, k_send, k_recv, (pl.ds(0, HALF), pl.ds(HALF, KROWS - HALF)))
    vm = moves(vb, v_send, v_recv, (pl.ds(0, BLOCK),))

    def when(cond, act):
        @pl.when(cond)
        def _():
            act()

    def send_first(m):
        when(core0, m["one_a"].start)
        for copy in m["hop1"]:
            when(has_next, copy.start)

    def pass_second(m, later):
        for copy in m["in2"]:
            when(has_prev, copy.wait_recv)
        when(core0 & has_prev, m["three_a"].start)
        when(core1 & has_prev, m["one_b"].start)
        for copy in m["hop2"]:
            when(passes & jnp.logical_not(later), copy.start)

    def hand_back(m):
        for arrived, back in zip(m["in4"], m["back2"]):
            arrived.wait_recv()
            back.start()
        for copy in m["hop2"]:
            copy.start()

    def take_third(m):
        for copy in m["in3"]:
            copy.wait_recv()
        m["four"].start()

    def take_fourth(m):
        for copy in m["in4"]:
            when(core0 & (s >= 4) & jnp.logical_not(hands_back), copy.wait_recv)
        when(core1 & (s >= 4), m["four"].wait_recv)

    q_copy.wait()
    sub = lax.broadcasted_iota(jnp.int32, (HD, BLOCK), 0)
    q_side = jnp.where(
        sub < 8, jnp.where(sub > depth, HIDE, 0.0), jnp.where(sub == 8, 1.0, 0.0)
    ).astype(BF16)
    qx[...] = q_side.T

    def key_side(slot):
        rows = kb[slot, BLOCK:, :].astype(F32)
        line = jnp.concatenate([rows[i : i + 1] for i in range(BLOCK // HD)], 1)
        off = jnp.where(mask_ref[0, slot] > 0, 0.0, HIDE).astype(F32)
        side = jnp.where(
            sub < 8, jnp.where(sub.astype(F32) == line, 1.0, 0.0), jnp.where(sub == 8, off, 0.0)
        ).astype(BF16)
        kx[...] = side.T

    half = HALF

    def spread_max(scores):
        return jnp.broadcast_to(
            jnp.max(lane_max(scores), axis=1, keepdims=True), (scores.shape[0], HD)
        )

    def own_scores():
        row = lax.broadcasted_iota(jnp.int32, (half, half), 0)
        col = lax.broadcasted_iota(jnp.int32, (half, half), 1)

        def heads(i, carry):
            for k in range(PER_BODY):
                h = i * PER_BODY + k
                cols = pl.ds(pl.multiple_of(h * HD, HD), HD)
                for t in range(2):
                    rs = slice(t * half, (t + 1) * half)
                    n = (t + 1) * half
                    scores = lax.dot_general(
                        qb[rs, cols], kb[0, :n], CONTRACT_LAST, preferred_element_type=F32
                    )
                    diag = jnp.where(col <= row, scores[:, n - half :], HIDE)
                    sc[h, 0, rs, n - half : n] = diag
                    best = lane_max(diag)
                    if t:
                        sc[h, 0, rs, : n - half] = scores[:, : n - half]
                        best = jnp.maximum(best, lane_max(scores[:, : n - half]))
                    mx[h, rs] = spread_max(best)
            return carry

        lax.fori_loop(0, HEADS // PER_BODY, heads, 0)

    def slot_scores(slot):
        key_side(slot)

        def heads(i, carry):
            keys = jnp.concatenate([kb[slot, :BLOCK], kx[...]], 1)
            for k in range(PER_BODY):
                h = i * PER_BODY + k
                cols = pl.ds(pl.multiple_of(h * HD, HD), HD)
                query = jnp.concatenate([qb[:, cols], qx[...]], 1)
                scores = lax.dot_general(query, keys, CONTRACT_LAST, preferred_element_type=F32)
                sc[h, slot] = scores
                mx[h] = jnp.maximum(mx[h], spread_max(scores))
            return carry

        lax.fori_loop(0, HEADS // PER_BODY, heads, 0)

    def store_result(h, rs, sums, top):
        cols = pl.ds(pl.multiple_of(h * HD, HD), HD)
        ob[rs, cols] = (sums[:, :HD] / sums[:, HD:]).astype(BF16)
        logs = top * SCALE + jnp.log(sums[:, HD:])
        l_ref[pl.ds(h, 1), rs] = logs[:, :1].reshape(1, half)

    def out_copy(i):
        cols = pl.ds(pl.multiple_of(i * (HEADS * HD // 2), HEADS * HD // 2), HEADS * HD // 2)
        return pltpu.make_async_copy(ob.at[:, cols], o_hbm.at[:, cols], local_sem.at[5 + i])

    def absorb(slots, first=False, last=False):
        per = HEADS
        steps = 2

        def heads(i, carry):
            for k in range(per):
                h = i * per + k
                for t in range(steps):
                    rs = slice(t * BLOCK // steps, (t + 1) * BLOCK // steps)
                    top = mx[h, rs]
                    sums = None
                    for slot in slots:
                        n = (t + 1) * half if first else BLOCK
                        terms = jnp.concatenate(
                            [
                                jnp.exp2(
                                    (sc[h, slot, rs, j * HD : (j + 1) * HD] - top) * SCALE_LOG2
                                ).astype(BF16)
                                for j in range(n // HD)
                            ],
                            1,
                        )
                        values = jnp.concatenate([vb[slot, :n], jnp.ones((n, HD), BF16)], 1)
                        part = jnp.dot(terms, values, preferred_element_type=F32)
                        sums = part if sums is None else sums + part
                    if not first:
                        fade = jnp.exp2((tops[h, rs] - top) * SCALE_LOG2)
                        sums = acc[h, rs] * jnp.concatenate([fade, fade], 1) + sums
                    if last:
                        store_result(h, rs, sums, top)
                    else:
                        acc[h, rs] = sums
                        tops[h, rs] = top
            if last:
                out_copy(0).start()
                out_copy(1).start()
            return carry

        lax.fori_loop(0, HEADS // per, heads, 0)

    def finish():
        def heads(i, carry):
            for k in range(HEADS // 2):
                h = i * (HEADS // 2) + k
                for t in range(2):
                    rs = slice(t * half, (t + 1) * half)
                    store_result(h, rs, acc[h, rs], tops[h, rs])
            out_copy(i).start()
            return carry

        lax.fori_loop(0, 2, heads, 0)

    def wait_spread(copies, own):
        own.wait()
        for copy in copies:
            copy.wait_recv()

    wait_spread(k_spread, k_own)
    send_first(km)
    own_scores()
    wait_spread(v_spread, v_own)
    send_first(vm)
    absorb((0,), first=True)

    @pl.when(s == 1)
    def _():
        vb[2] = jnp.zeros((BLOCK, HD), BF16)

        def fill(h, carry):
            sc[h, 2] = jnp.full((BLOCK, BLOCK), HIDE, F32)
            return carry

        lax.fori_loop(0, HEADS, fill, 0)

    def by_round(r, first_core, second_core):
        pick = jnp.int32(0)
        for i in range(len(first_core)):
            pick = jnp.where(r == i, jnp.where(core0, first_core[i], second_core[i]), pick)
        return pick

    def round_of(r, carry):
        def at(i, cond, act):
            when((r == i) & cond, act)

        plain0 = core0 & jnp.logical_not(relayed)
        at(0, core1, km["one_a"].wait_recv)
        at(1, jnp.logical_not(relayed), lambda: pass_second(km, hands_back))
        at(1, relayed, km["one_a"].wait_recv)
        at(2, hands_back, lambda: hand_back(km))
        at(2, relayed, lambda: pass_second(km, hands_back))
        at(2, jnp.logical_not(relayed), lambda: pass_second(vm, hands_back | skips))
        at(2, plain0 & (s >= 1), km["one_a"].wait_recv)
        at(3, hands_back, lambda: hand_back(vm))
        at(3, core0 & (s >= 4), lambda: take_third(km))
        at(3, core1 & (s >= 3), vm["three_a"].wait_recv)
        at(4, skips & passes, vm["hop2"][0].start)
        at(4, relayed, lambda: pass_second(vm, hands_back))
        at(5, core0 & (s >= 4), lambda: take_third(vm))
        pairs = (r == jnp.where(core1, 2, jnp.where(relayed, 4, 5))) & (s >= 1)
        when(pairs, vm["one_a"].wait_recv)
        when(pairs, lambda: absorb((1, 2)))
        thirds = ((r == 3) & core1 & (s >= 3)) | ((r == 5) & relayed)
        when(thirds, lambda: absorb((3,)))
        at(2, core1 & (s >= 3), km["three_a"].wait_recv)
        at(3, core1, lambda: take_fourth(km))
        at(4, core0, lambda: take_fourth(km))
        slot = by_round(
            r,
            tuple(jnp.where(relayed, i, j) for i, j in ((0, 0), (1, 2), (2, 1), (3, 3), (4, 4))),
            (1, 2, 3, 4, 0),
        )

        @pl.when((slot > 0) & (slot <= s))
        def _():
            slot_scores(slot)

        return carry

    lax.fori_loop(0, 6, round_of, 0)
    take_fourth(vm)
    both = core0 & jnp.logical_not(relayed)
    when((s >= 4) & both, lambda: absorb((3, 4), last=True))
    when((s >= 4) & jnp.logical_not(both), lambda: absorb((4,), last=True))
    when(s < 4, finish)
    for i in range(2):
        out_copy(i).wait()

    for copy in k_spread + v_spread:
        copy.wait_send()
    for m in (km, vm):
        for i in range(len(m["hop1"])):
            when(has_next, m["hop1"][i].wait_send)
            when(passes, m["hop2"][i].wait_send)
            when(hands_back, m["back2"][i].wait_send)
        when(core0 | has_prev, m["one_a"].wait_send)
        when(core0 & has_prev, m["three_a"].wait_send)
        when(core0 & (s >= 4), m["four"].wait_send)


def copy_out(a_in, l_in, a_out, l_out, a_buf, l_buf, sem_in, sem_out):
    rows = BLOCK // PIECES
    pieces = [pl.ds(i * rows, rows) for i in range(PIECES)]
    loads = [
        pltpu.make_async_copy(a_in.at[p], a_buf.at[p], sem_in.at[i]) for i, p in enumerate(pieces)
    ] + [pltpu.make_async_copy(l_in, l_buf, sem_in.at[PIECES])]
    stores = [
        pltpu.make_async_copy(a_buf.at[p], a_out.at[p], sem_out.at[i])
        for i, p in enumerate(pieces)
    ] + [pltpu.make_async_copy(l_buf, l_out, sem_out.at[PIECES])]
    for load in loads:
        load.start()
    for load, store in zip(loads, stores):
        load.wait()
        store.start()
    for store in stores:
        store.wait()


def solution(mesh):
    blocks = mesh.shape["seq"]

    def body(query_rows, key_rows, value_rows, tree_mask, token_depth):
        vmem = pl.BlockSpec(memory_space=pltpu.VMEM)
        anywhere = pl.BlockSpec(memory_space=pl.ANY)
        sems = pltpu.SemaphoreType.DMA
        results = pl.pallas_call(
            functools.partial(kernel, blocks),
            out_shape=(
                jax.ShapeDtypeStruct((BLOCK, HEADS * HD), BF16),
                jax.ShapeDtypeStruct((HEADS, BLOCK), F32),
            ),
            in_specs=[anywhere] * 5,
            out_specs=(anywhere, vmem),
            scratch_shapes=[
                pltpu.SMEM((1, SLOTS), jnp.int32),
                pltpu.VMEM((1, BLOCK), jnp.int32),
                pltpu.VMEM((ROWS, GROUP * HD), BF16),
                pltpu.VMEM((ROWS, GROUP * HD), BF16),
                pltpu.VMEM((BLOCK, HEADS * HD), BF16),
                pltpu.VMEM((BLOCK, HEADS * HD), BF16),
                pltpu.VMEM((SLOTS, KROWS, HD), BF16),
                pltpu.VMEM((SLOTS, BLOCK, HD), BF16),
                pltpu.VMEM((BLOCK, HD), BF16),
                pltpu.VMEM((BLOCK, HD), BF16),
                pltpu.VMEM((HEADS, SLOTS, BLOCK, BLOCK), F32),
                pltpu.VMEM((HEADS, BLOCK, HD), F32),
                pltpu.VMEM((HEADS, BLOCK, HD), F32),
                pltpu.VMEM((HEADS, BLOCK, 2 * HD), F32),
                sems((16,)), sems((16,)), sems((16,)), sems((16,)), sems((9,)),
            ],
            compiler_params=pltpu.CompilerParams(
                collective_id=0, has_side_effects=True, vmem_limit_bytes=60 * 2**20
            ),
        )(query_rows, key_rows, value_rows, tree_mask, token_depth.reshape(1, BLOCK))
        return pl.pallas_call(
            copy_out,
            out_shape=tuple(jax.ShapeDtypeStruct(r.shape, r.dtype) for r in results),
            in_specs=[anywhere] * 2,
            out_specs=(anywhere,) * 2,
            scratch_shapes=[
                pltpu.VMEM((BLOCK, HEADS * HD), BF16),
                pltpu.VMEM((HEADS, BLOCK), F32),
                sems((PIECES + 1,)),
                sems((PIECES + 1,)),
            ],
            compiler_params=pltpu.CompilerParams(vmem_limit_bytes=60 * 2**20),
        )(*results)

    return jax.shard_map(
        body,
        mesh=mesh,
        in_specs=(
            P("seq", "head"),
            P(("seq", "head"), None),
            P(("seq", "head"), None),
            P("seq", None),
            P("seq"),
        ),
        out_specs=(P("seq", "head"), P("head", "seq")),
        check_vma=False,
    )
```
